512 devices in a mesh: dp: 32 (over z, core), tensor: 16 (over x, y).
Axes of the slice: x: 4, y: 4, z: 16, core: 2. Of those that a mesh axis runs over, the one named last changes fastest.
Arguments:
- activations: bfloat16 [16384, 8192], P('dp', 'tensor'), may hold values from -6 to 6
- kv_weight: bfloat16 [8192, 2048], P('tensor'), may hold values from -0.09375 to 0.09375
- pool_shrink: bfloat16 [128, 64, 8192], P('dp', None, 'tensor'), may hold values from -0.0625 to 0.0625
- pool_expand: bfloat16 [128, 64, 2048], P('dp', None, 'tensor'), may hold values from -0.75 to 0.75
- request_slot: int32 [16384], P('dp'), may hold values from 0 to 31
- slot_owner: int32 [1024, 1], P('dp'), may hold values from 0 to 31; in each aligned block of 32 rows (0 to 31, 32 to 63, ...) at most 2 rows name the same one
- slot_local: int32 [1024, 1], P('dp'), may hold values from 0 to 3
Outputs:
- projected: bfloat16 [16384, 2048], P('dp', 'tensor')
The draws below stay inside these ranges and needn't reach their ends.
Inputs may be any that keep to these rules, and one draw needn't show every extreme that they name: `slot_owner`: among the 32 slots of one group (an aligned block of 32 rows) no owner appears more than 2 times, and some owner appears exactly 2 times in some group.
All inputs are finite; a program needn't handle non-finite values.
Results may differ from the reference program's by a relative error of at most 0.0037.
Values may be sent and summed in bfloat16 or wider, within the bound.
A program may use at most 64 MiB of HBM per device.

```python
import math
import jax
import jax.numpy as jnp
import numpy as np
from jax import lax

D = 8192
KVW = 2048
RANK = 64
CAP = 2
POOL_DEV = 4
REQ_GROUP = 512
GROUPS = 32
SLOTS = 32
REQS = 16384
POOL = 128


def touch_ends(entries, key, low, largest):
    shape = entries.shape
    index_at = [jax.random.randint(jax.random.fold_in(key, axis), (), 0, shape[axis]) for axis in range(len(shape))]
    entries = entries.at[tuple(index_at)].set(low)
    longest = shape.index(max(shape))
    index_at[longest] = (index_at[longest] + 1) % shape[longest]
    return entries.at[tuple(index_at)].set(largest)


def raised(values, key, source, target, parts, factor):
    def block_of(dim):
        return (jnp.arange(values.shape[dim]) // (values.shape[dim] // parts)).reshape((-1,) + (1,) * (values.ndim - 1 - dim))

    first = jax.random.permutation(key, parts)[block_of(target)]
    second = (block_of(target) + parts // 2) % parts
    return jnp.where((block_of(source) == first) | (block_of(source) == second), factor * values, values)


def shard_levels(stream_key, extent, shards, low, high):
    level = 1.0
    for dim, shards_of in shards:
        heights = jax.random.uniform(jax.random.fold_in(jax.random.fold_in(stream_key, 6), dim), (shards_of,), jnp.float32, low / len(shards), high / len(shards))
        level = level * jnp.repeat(jnp.exp(heights), extent[dim] // shards_of).reshape((-1,) + (1,) * (len(extent) - 1 - dim))
    return level


def rank_bounds(amount, lean):
    loads = [(1 << 20) // math.isqrt(grade ** lean) + 1 for grade in range(1, amount + 1)]
    deviation = 1 + sum(loads) // (1 << 30)
    return np.cumsum(np.array([max(1, weight // deviation) for weight in loads]))


def ranked(own_key, extent, amount, slope):
    listing = rank_bounds(amount, slope)
    pick = jax.random.randint(jax.random.fold_in(own_key, 1), extent, 0, int(listing[amount - 1]))
    rank = jnp.searchsorted(jnp.asarray(listing, jnp.int32), pick, side="right")
    return jax.random.permutation(jax.random.fold_in(own_key, 2), amount)[rank].astype(jnp.int32)


def routed_block(rng, own, number, rows, number_of, top, bound, slope):
    order = jax.random.permutation(rng, number_of)
    heavy_load, usual = shares(number_of, rows * top, bound, slope, True), shares(number_of, rows * top, bound, slope, False)
    places = jnp.arange(number_of)

    def named(lengths, turn):
        used = int((lengths > 0).sum())
        fixed = max(1, used // 4)
        shifted = fixed + (places - fixed + turn * (used - fixed)) % max(1, number_of - fixed)
        return jnp.zeros((number_of,), jnp.int32).at[order[jnp.where(places < fixed, places, shifted)]].set(jnp.asarray(lengths, jnp.int32))

    lengths = jnp.where(number % 4 == 0, named(heavy_load, number // 4), named(usual, number - number // 4 - 1))
    mixed = jax.random.permutation(jax.random.fold_in(own, 3), number_of)
    source_of, receiver = mixed[0:number_of // 2 * 2:2], mixed[1:number_of // 2 * 2:2]
    slack = jnp.minimum(lengths[source_of] - 1, bound - lengths[receiver]) // 2
    slack = jnp.where((source_of == order[0]) | (receiver == order[0]) | (lengths[receiver] == 0), 0, jnp.maximum(slack, 0))
    shifted = jax.random.randint(jax.random.fold_in(own, 4), (number_of // 2,), 0, 1 << 20) % (slack + 1)
    lengths = lengths.at[source_of].add(-shifted).at[receiver].add(shifted)
    items = jnp.searchsorted(jnp.cumsum(lengths), jnp.arange(rows * top), side="right").astype(jnp.int32)
    grid = items.reshape(top, rows).T
    grid = grid[jax.random.permutation(jax.random.fold_in(own, 1), rows)]
    turn = jax.random.randint(jax.random.fold_in(own, 2), (rows, 1), 0, top)
    return jnp.take_along_axis(grid, (jnp.arange(top)[None, :] + turn) % top, axis=1)


def shares(amount, total, limit, slope, full):
    portions = [(1 << 20) // math.isqrt(standing ** slope) + 1 for standing in range(1, amount + 1)]
    largest = limit if full else min(limit, max(-(-total // amount), total * portions[0] // sum(portions)))
    least = 1 if total - largest >= amount - 1 else 0
    given, rest = [largest] + [least] * (amount - 1), total - largest - least * (amount - 1)
    while rest > 0:
        free = [i for i in range(1, amount) if given[i] < largest] or [i for i in range(1, amount) if given[i] < limit]
        mass, left = sum([portions[i] for i in free]), rest
        for i in free:
            more = min(limit - given[i], max(1, left * portions[i] // mass), rest)
            given[i] = given[i] + more
            rest = rest - more
    return np.array(given)


def centred(key, shape, width, most, pieces=(), held_as=jnp.bfloat16):
    level = shard_levels(key, shape, pieces, -0.22, 0.18) if pieces else 1.0
    drawn = jax.random.normal(key, shape, jnp.float32) * width * level
    return jnp.minimum(jnp.maximum(drawn, -most), most).astype(held_as)


def heavy_noise(stream_key, extent, width, most, shards, heavy, kind=jnp.bfloat16):
    drawn = width * jax.random.normal(stream_key, extent, jnp.float32)
    if shards:
        drawn = drawn * shard_levels(stream_key, extent, shards, -0.22, 0.18)
    return jnp.clip(raised(drawn, jax.random.fold_in(stream_key, 3), *heavy), -most, most).astype(kind)


def setup_inputs(seed: int = 0) -> dict:
    seeds = jax.random.split(jax.random.key(seed), 8)
    activations = centred(seeds[0], (REQS, D), 1.0, 6.0, ((0, 32), (1, 16)))
    kv_weight = heavy_noise(seeds[1], (D, KVW), D ** -0.5, 0.09375, ((0, 16),), (0, 1, 16, 2.0))
    pool_shrink = centred(seeds[2], (POOL, RANK, D), D ** -0.5, 0.0625, ((0, 32), (2, 16)))
    pool_expand = centred(seeds[3], (POOL, RANK, KVW), RANK ** -0.5, 0.75, ((0, 32), (2, 16)))
    request_slot = touch_ends(ranked(seeds[4], (REQS,), SLOTS, 2), jax.random.fold_in(seeds[4], 3), 0, SLOTS - 1).astype(jnp.int32)
    slot_owner_keys = jax.random.split(jax.random.fold_in(seeds[5], 1), (GROUPS * SLOTS) // SLOTS)
    slot_owner_turns = jax.random.permutation(jax.random.fold_in(seeds[5], 3), (GROUPS * SLOTS) // SLOTS)
    slot_owner = jax.vmap(lambda own, number: routed_block(jax.random.fold_in(seeds[5], 2), own, number, SLOTS, GROUPS, 1, CAP, 2))(slot_owner_keys, slot_owner_turns).reshape((GROUPS * SLOTS, 1))
    slot_local = touch_ends(jax.random.randint(seeds[6], (GROUPS * SLOTS, 1), 0, POOL_DEV), jax.random.fold_in(seeds[6], 1), 0, POOL_DEV - 1).astype(jnp.int32)
    return dict(activations=activations, kv_weight=kv_weight, pool_shrink=pool_shrink, pool_expand=pool_expand, request_slot=request_slot, slot_owner=slot_owner, slot_local=slot_local)


def reference(activations, kv_weight, pool_shrink, pool_expand, request_slot, slot_owner, slot_local):
    def one_group(packed):
        group_rows, group_slots, group_owner, group_local = packed
        pool_row = group_owner * POOL_DEV + group_local
        shrink_rows = pool_shrink[pool_row].reshape(SLOTS * RANK, D)
        expand_rows = pool_expand[pool_row].reshape(SLOTS * RANK, KVW)
        base_part = jnp.dot(group_rows, kv_weight, preferred_element_type=jnp.float32)
        all_shrunk = lax.dot_general(group_rows, shrink_rows, (((1,), (1,)), ((), ())), preferred_element_type=jnp.float32)
        chosen = group_slots[:, None] == jnp.arange(SLOTS, dtype=jnp.int32)[None, :]
        picked = jnp.where(chosen[:, :, None], all_shrunk.reshape(-1, SLOTS, RANK), jnp.zeros((), jnp.float32))
        shrunk = jnp.sum(picked, axis=1).astype(jnp.bfloat16)
        widened = jnp.where(chosen[:, :, None], shrunk[:, None, :], jnp.zeros((), jnp.bfloat16)).reshape(-1, SLOTS * RANK)
        adapted = jnp.dot(widened, expand_rows, preferred_element_type=jnp.float32)
        return (base_part + adapted).astype(jnp.bfloat16)

    packed = (activations.reshape(GROUPS, REQ_GROUP, D),
              request_slot.reshape(GROUPS, REQ_GROUP),
              slot_owner.reshape(GROUPS, SLOTS),
              slot_local.reshape(GROUPS, SLOTS))
    result = lax.map(one_group, packed)
    return result.reshape(REQS, KVW)
```

```python
import functools

import jax
import jax.numpy as jnp
from jax import lax
from jax.experimental import pallas as pl
from jax.experimental.pallas import tpu as pltpu
from jax.sharding import PartitionSpec as P

MESH = pl.DeviceIdType.MESH
BF16, F32 = jnp.bfloat16, jnp.float32
PLANES, CORES, XS, YS = 16, 2, 4, 4
OWNERS, PEERS = PLANES * CORES, XS * YS
HELD, RANK, SLOTS = 4, 64, 32
REQ, WIDTH, FEAT = 512, 512, 128
HALF = PLANES // 2
ORDERS = ((0, 1, 2, 3), (2, 3, 0, 1))
KEPT = ((0, 1), (2, 3))
EXPAND_LATE = 5


def away(offset):
    return sum(min(step, 4 - step) for step in offset)


OFFSETS = sorted(((i, j) for i in range(XS) for j in range(YS) if i or j), key=lambda offset: -away(offset))


def remote(src, dst, send, recv, device):
    return pltpu.make_async_remote_copy(
        src_ref=src, dst_ref=dst, send_sem=send, recv_sem=recv, device_id=device, device_id_type=MESH
    )


def kernel(
    owners, locals_, slots, act_hbm, kv_hbm, shrink_hbm, expand_hbm, out,
    act, act_t, kv, shrinks, expands, part_out, part_in, base, adapter, picked, sum_in, sum_own, shrunk_t, hot, rows,
    load, ring_send, ring_recv, sib_send, sib_recv, up_send, up_recv, upsib_send, upsib_recv,
    base_send, base_recv, sum_send, sum_recv, all_send, all_recv,
):
    dp, tensor = lax.axis_index("dp"), lax.axis_index("tensor")
    z, core = dp // CORES, dp % CORES
    x, y = tensor // YS, tensor % YS

    def owner_at(way, hop, which=core):
        plane = (z - hop + PLANES) % PLANES if way == 0 else (z + hop) % PLANES
        return plane * CORES + which

    next_of = ({"dp": owner_at(1, 1)}, {"dp": owner_at(0, 1)})
    sibling = {"dp": z * CORES + 1 - core}

    def peer(offset, sign=1):
        other_x = (x + sign * offset[0] + XS) % XS
        other_y = (y + sign * offset[1] + YS) % YS
        return other_x, other_y

    def peer_id(offset, sign=1):
        other_x, other_y = peer(offset, sign)
        return {"tensor": other_x * YS + other_y}

    loads = [
        pltpu.make_async_copy(act_hbm, act, load.at[0]),
        pltpu.make_async_copy(kv_hbm, kv, load.at[1]),
        pltpu.make_async_copy(shrink_hbm, shrinks.at[dp], load.at[2]),
        pltpu.make_async_copy(expand_hbm, expands.at[dp], load.at[3]),
    ]
    for copy in loads:
        copy.start()

    barrier = pltpu.get_barrier_semaphore()
    for device in (next_of[0], next_of[1], sibling):
        pl.semaphore_signal(barrier, inc=1, device_id=device, device_id_type=MESH)
    for offset in OFFSETS:
        pl.semaphore_signal(barrier, inc=1, device_id=peer_id(offset), device_id_type=MESH)
    pl.semaphore_wait(barrier, 3 + len(OFFSETS))

    def ring_copy(way, hop, chunk, src):
        return remote(
            src, shrinks.at[owner_at(way, hop), chunk], ring_send.at[way, hop, chunk],
            ring_recv.at[way, hop, chunk], next_of[way],
        )

    def ring_forward(way, hop, chunk):
        ring_copy(way, hop, chunk, shrinks.at[owner_at(way, hop), chunk]).start()

    def ring_arrived(way, hop, chunk):
        owner = owner_at(way, hop)
        remote(
            shrinks.at[owner, chunk], shrinks.at[owner, chunk], ring_send.at[way, hop, chunk],
            ring_recv.at[way, hop - 1, chunk], next_of[way],
        ).wait_recv()

    def sib_copy(way, hop, which):
        shard = shrinks.at[owner_at(way, hop, which)]
        return remote(shard, shard, sib_send.at[way, hop], sib_recv.at[way, hop], sibling)

    def sib_half(way, which):
        shard = shrinks.at[owner_at(way, HALF, which), pl.ds(2 * way, 2)]
        return remote(shard, shard, sib_send.at[way, HALF], sib_recv.at[way, HALF], sibling)

    def up_part(way, hop):
        return pl.ds(2 * way, 2) if hop == HALF else pl.ds(0, HELD)

    def up_copy(way, hop, owner, piece):
        part = expands.at[owner, pl.ds(2 * piece, 2)]
        return remote(part, part, up_send.at[way, hop, piece], up_recv.at[way, hop, piece], next_of[way])

    def up_forward(way, hop):
        for piece in (way, 1 - way):
            if hop < HALF - 1 or piece == way:
                up_copy(way, hop, owner_at(way, hop), piece).start()

    def upsib_copy(way, hop, which):
        shard = expands.at[owner_at(way, hop, which), up_part(way, hop)]
        return remote(shard, shard, upsib_send.at[way, hop], upsib_recv.at[way, hop], sibling)

    def up_hop(hop):
        for way in (0, 1):
            for piece in (way, 1 - way):
                if hop < HALF or piece == way:
                    up_copy(way, hop - 1, owner_at(way, hop), piece).wait_recv()
                    if hop < HALF - 1 or (hop == HALF - 1 and piece == way):
                        up_copy(way, hop, owner_at(way, hop), piece).start()
            upsib_copy(way, hop, core).start()

    for place in range(HELD):
        for way in (0, 1):
            chunk = ORDERS[way][place]
            ring_copy(way, 0, chunk, shrink_hbm.at[chunk]).start()

    loads[0].wait()
    loads[1].wait()

    def base_block(pair, carry):
        both = jnp.dot(act[...], kv[:, pl.ds(pl.multiple_of(pair * 2 * FEAT, 2 * FEAT), 2 * FEAT)], preferred_element_type=F32)
        part_out[2 * pair] = both[:, :FEAT].astype(BF16)
        part_out[2 * pair + 1] = both[:, FEAT:].astype(BF16)
        return carry

    lax.fori_loop(0, PEERS // 2, base_block, 0)

    def base_copy(index):
        offset = OFFSETS[index]
        other_x, other_y = peer(offset)
        return remote(
            part_out.at[other_x * YS + other_y], part_in.at[index], base_send.at[index], base_recv.at[index], peer_id(offset)
        )

    for index in range(len(OFFSETS)):
        base_copy(index).start()
    base[...] = jnp.dot(
        act[...], kv[:, pl.ds(pl.multiple_of(tensor * FEAT, FEAT), FEAT)], preferred_element_type=F32
    )

    loads[2].wait()
    loads[3].wait()
    sib_copy(0, 0, core).start()
    slot_row = slots[...]
    named = jnp.zeros((1, REQ), jnp.int32)
    for slot in range(SLOTS):
        named = jnp.where(slot_row == slot, owners[slot] * HELD + locals_[slot], named)
    adapter[...] = jnp.broadcast_to(named, adapter.shape)
    act_t[...] = act[...].T
    slot_column = jnp.broadcast_to(slot_row, (FEAT, REQ)).T
    lane_slot = lax.broadcasted_iota(jnp.int32, (REQ, FEAT), 1) // RANK
    for pair in range(SLOTS // 2):
        hot[:, pair * FEAT : (pair + 1) * FEAT] = jnp.where(slot_column == lane_slot + 2 * pair, 1.0, 0.0).astype(BF16)
    picked[...] = jnp.zeros_like(picked)

    def shrink_with(owner, first=0, count=HELD):
        weights = shrinks[owner, pl.ds(first, count)].reshape(count * RANK, WIDTH)
        block = jnp.dot(weights, act_t[...], preferred_element_type=F32)
        total = picked[...]
        for local in range(count):
            hit = adapter[0:1, :] == owner * HELD + first + local
            total = jnp.where(hit, block[local * RANK : (local + 1) * RANK], total)
        picked[...] = total

    def add_base(index):
        base_copy(index).wait_recv()
        base[...] += part_in[index].astype(F32)

    def work(place, hop):
        way = place % 2
        if place < 2:
            shrink_with(owner_at(way, hop))
        elif way == 0:
            sib_copy(0, hop, 1 - core).wait_recv()
            shrink_with(owner_at(0, hop, 1 - core))
        else:
            @pl.when(hop > 0)
            def _():
                sib_copy(1, hop, 1 - core).wait_recv()

            shrink_with(owner_at(1, hop, 1 - core))

    def shrink_hop(hop, carry):
        for place in range(HELD):
            for way in (0, 1):
                chunk = ORDERS[way][place]
                ring_arrived(way, hop, chunk)
                if chunk in KEPT[way]:
                    ring_forward(way, hop, chunk)
                else:
                    pl.when(hop < HALF - 1)(functools.partial(ring_forward, way, hop, chunk))
            work(place, hop - 1)
        for way in (0, 1):
            sib_copy(way, hop, core).start()
        return carry

    lax.fori_loop(1, 4, shrink_hop, 0)
    up_forward(0, 0)
    up_forward(1, 0)
    upsib_copy(0, 0, core).start()
    for hop in range(4, HALF):
        shrink_hop(hop, 0)
        up_hop(hop - 3)
        if hop >= 5:
            for index in range(5 * (hop - 5), 5 * (hop - 4)):
                add_base(index)
    for place in (0, 1):
        for way in (0, 1):
            ring_arrived(way, HALF, ORDERS[way][place])
    for way in (0, 1):
        sib_half(way, core).start()
    up_hop(EXPAND_LATE)
    for place in range(HELD):
        work(place, HALF - 1)
    for way in (0, 1):
        shrink_with(owner_at(way, HALF), 2 * way, 2)
    for way in (0, 1):
        sib_half(way, 1 - core).wait_recv()
        shrink_with(owner_at(way, HALF, 1 - core), 2 * way, 2)

    def piece_of(ref, at_x, at_y):
        return ref.at[pl.ds(pl.multiple_of(at_x * 16, 16), 16), pl.ds(pl.multiple_of(at_y * 128, 128), 128)]

    def sum_copy(index):
        other_x, other_y = peer(OFFSETS[index])
        return remote(
            piece_of(picked, other_x, other_y), sum_in.at[index], sum_send.at[index], sum_recv.at[index], peer_id(OFFSETS[index])
        )

    def all_copy(index, sign=1):
        at_x, at_y = (x, y) if sign == 1 else peer(OFFSETS[index], -1)
        return remote(
            piece_of(shrunk_t, at_x, at_y), piece_of(shrunk_t, at_x, at_y), all_send.at[index], all_recv.at[index],
            peer_id(OFFSETS[index]),
        )

    for index in range(len(OFFSETS)):
        sum_copy(index).start()
    up_hop(6)
    total = piece_of(picked, x, y)[...]
    for index in reversed(range(len(OFFSETS))):
        sum_copy(index).wait_recv()
        total += sum_in[index]
    piece_of(shrunk_t, x, y)[...] = total.astype(BF16)
    for index in range(len(OFFSETS)):
        all_copy(index).start()
    up_hop(7)
    for index in reversed(range(len(OFFSETS))):
        all_copy(index, -1).wait_recv()
    twice = jnp.concatenate([shrunk_t[...], shrunk_t[...]], axis=0).T
    for pair in range(SLOTS // 2):
        hot[:, pair * FEAT : (pair + 1) * FEAT] *= twice
    up_hop(HALF)
    upsib_copy(0, 0, 1 - core).wait_recv()
    for hop in range(1, HALF + 1):
        for way in (0, 1):
            upsib_copy(way, hop, 1 - core).wait_recv()
    for slot in range(SLOTS):
        rows[slot * RANK : (slot + 1) * RANK, :] = expands[owners[slot], locals_[slot]]
    out[...] = (base[...] + jnp.dot(hot[...], rows[...], preferred_element_type=F32)).astype(BF16)

    for way in (0, 1):
        for hop in range(HALF):
            for chunk in range(HELD):
                if hop < HALF - 1 or chunk in KEPT[way]:
                    ring_copy(way, hop, chunk, shrinks.at[owner_at(way, hop), chunk]).wait_send()
            for piece in (0, 1):
                if hop < HALF - 1 or piece == way:
                    up_copy(way, hop, owner_at(way, hop), piece).wait_send()
        for hop in range(HALF + 1):
            if hop or way == 0:
                (sib_half(way, core) if hop == HALF else sib_copy(way, hop, core)).wait_send()
                upsib_copy(way, hop, core).wait_send()
    for index in range(len(OFFSETS)):
        base_copy(index).wait_send()
        sum_copy(index).wait_send()
        all_copy(index).wait_send()


def shards(activations, kv_weight, pool_shrink, pool_expand, request_slot, slot_owner, slot_local):
    peers = len(OFFSETS)
    dma = pltpu.SemaphoreType.DMA
    hbm = pl.BlockSpec(memory_space=pl.ANY)
    smem = pl.BlockSpec(memory_space=pltpu.SMEM)
    vmem = pl.BlockSpec(memory_space=pltpu.VMEM)
    return pl.pallas_call(
        kernel,
        out_shape=jax.ShapeDtypeStruct((REQ, FEAT), BF16),
        in_specs=[smem, smem, vmem, hbm, hbm, hbm, hbm],
        out_specs=vmem,
        scratch_shapes=[
            pltpu.VMEM((REQ, WIDTH), BF16),
            pltpu.VMEM((WIDTH, REQ), BF16),
            pltpu.VMEM((WIDTH, PEERS * FEAT), BF16),
            pltpu.VMEM((OWNERS, HELD, RANK, WIDTH), BF16),
            pltpu.VMEM((OWNERS, HELD, RANK, FEAT), BF16),
            pltpu.VMEM((PEERS, REQ, FEAT), BF16),
            pltpu.VMEM((peers, REQ, FEAT), BF16),
            pltpu.VMEM((REQ, FEAT), F32),
            pltpu.VMEM((8, REQ), jnp.int32),
            pltpu.VMEM((RANK, REQ), F32),
            pltpu.VMEM((peers, 16, 128), F32),
            pltpu.VMEM((16, 128), F32),
            pltpu.VMEM((RANK, REQ), BF16),
            pltpu.VMEM((REQ, SLOTS * RANK), BF16),
            pltpu.VMEM((SLOTS * RANK, FEAT), BF16),
            dma((4,)),
            dma((2, HALF, HELD)),
            dma((2, HALF, HELD)),
            dma((2, HALF + 1)),
            dma((2, HALF + 1)),
            dma((2, HALF, 2)),
            dma((2, HALF, 2)),
            dma((2, HALF + 1)),
            dma((2, HALF + 1)),
            dma((peers,)),
            dma((peers,)),
            dma((peers,)),
            dma((peers,)),
            dma((peers,)),
            dma((peers,)),
        ],
        compiler_params=pltpu.CompilerParams(
            collective_id=0, has_side_effects=True, vmem_limit_bytes=40 * 2**20
        ),
    )(
        slot_owner.reshape(-1), slot_local.reshape(-1), request_slot.reshape(1, -1),
        activations, kv_weight, pool_shrink, pool_expand,
    )


def solution(mesh):
    in_specs = (
        P("dp", "tensor"),
        P("tensor", None),
        P("dp", None, "tensor"),
        P("dp", None, "tensor"),
        P("dp"),
        P("dp", None),
        P("dp", None),
    )
    out_specs = P("dp", "tensor")
    return jax.shard_map(shards, mesh=mesh, in_specs=in_specs, out_specs=out_specs, check_vma=False)
```

```python
import functools

import jax
import jax.numpy as jnp
from jax import lax
from jax.experimental import pallas as pl
from jax.experimental.pallas import tpu as pltpu
from jax.sharding import PartitionSpec as P

MESH = pl.DeviceIdType.MESH
BF16, F32 = jnp.bfloat16, jnp.float32
PLANES, CORES, XS, YS = 16, 2, 4, 4
OWNERS, PEERS = PLANES * CORES, XS * YS
HELD, RANK, SLOTS = 4, 64, 32
REQ, WIDTH, FEAT = 512, 512, 128
HALF = PLANES // 2
ORDERS = ((0, 1, 2, 3), (2, 3, 0, 1))
KEPT = ((0, 1), (2, 3))
EXPAND_LATE = 4


def away(offset):
    return sum(min(step, 4 - step) for step in offset)


OFFSETS = sorted(((i, j) for i in range(XS) for j in range(YS) if i or j), key=lambda offset: -away(offset))


def remote(src, dst, send, recv, device):
    return pltpu.make_async_remote_copy(
        src_ref=src, dst_ref=dst, send_sem=send, recv_sem=recv, device_id=device, device_id_type=MESH
    )


def kernel(
    owners_hbm, locals_hbm, slots_hbm, act_hbm, kv_hbm, shrink_hbm, expand_hbm, out,
    owners, locals_, slots, act, act_t, kv, shrinks, expands, part_out, part_in, base, adapter, picked, sum_in, shrunk_t, hot, rows,
    load, ring_send, ring_recv, sib_send, sib_recv, up_send, up_recv, upsib_send, upsib_recv,
    base_send, base_recv, sum_send, sum_recv, all_send, all_recv,
):
    dp, tensor = lax.axis_index("dp"), lax.axis_index("tensor")
    z, core = dp // CORES, dp % CORES
    x, y = tensor // YS, tensor % YS

    def owner_at(way, hop, which=core):
        plane = (z - hop + PLANES) % PLANES if way == 0 else (z + hop) % PLANES
        return plane * CORES + which

    next_of = ({"dp": owner_at(1, 1)}, {"dp": owner_at(0, 1)})
    after_next = ({"dp": owner_at(1, 2)}, {"dp": owner_at(0, 2)})
    sibling = {"dp": z * CORES + 1 - core}

    def peer(offset, sign=1):
        other_x = (x + sign * offset[0] + XS) % XS
        other_y = (y + sign * offset[1] + YS) % YS
        return other_x, other_y

    def peer_id(offset, sign=1):
        other_x, other_y = peer(offset, sign)
        return {"tensor": other_x * YS + other_y}

    loads = [
        pltpu.make_async_copy(act_hbm, act, load.at[0]),
        pltpu.make_async_copy(kv_hbm, kv, load.at[1]),
        pltpu.make_async_copy(shrink_hbm, shrinks.at[dp], load.at[2]),
        pltpu.make_async_copy(expand_hbm, expands.at[dp], load.at[3]),
        pltpu.make_async_copy(owners_hbm, owners, load.at[4]),
        pltpu.make_async_copy(locals_hbm, locals_, load.at[5]),
        pltpu.make_async_copy(slots_hbm, slots, load.at[6]),
    ]
    barrier = pltpu.get_barrier_semaphore()
    for device in (*next_of, *after_next, sibling):
        pl.semaphore_signal(barrier, inc=1, device_id=device, device_id_type=MESH)
    for offset in OFFSETS:
        pl.semaphore_signal(barrier, inc=1, device_id=peer_id(offset), device_id_type=MESH)
    for copy in loads:
        copy.start()
    pl.semaphore_wait(barrier, 5 + len(OFFSETS))

    def ring_copy(way, hop, chunk, src):
        return remote(
            src, shrinks.at[owner_at(way, hop), chunk], ring_send.at[way, hop, chunk],
            ring_recv.at[way, hop, chunk], next_of[way],
        )

    def ring_forward(way, hop, chunk):
        ring_copy(way, hop, chunk, shrinks.at[owner_at(way, hop), chunk]).start()

    def ring_arrived(way, hop, chunk):
        owner = owner_at(way, hop)
        remote(
            shrinks.at[owner, chunk], shrinks.at[owner, chunk], ring_send.at[way, hop, chunk],
            ring_recv.at[way, hop - 1, chunk], next_of[way],
        ).wait_recv()

    def sib_copy(way, hop, which):
        shard = shrinks.at[owner_at(way, hop, which)]
        return remote(shard, shard, sib_send.at[way, hop], sib_recv.at[way, hop], sibling)

    def sib_half(way, which):
        shard = shrinks.at[owner_at(way, HALF, which), pl.ds(2 * way, 2)]
        return remote(shard, shard, sib_send.at[way, HALF], sib_recv.at[way, HALF], sibling)

    def up_part(way, hop):
        return pl.ds(2 * way, 2) if hop == HALF else pl.ds(0, HELD)

    def up_copy(way, hop, owner, piece, step=1):
        part = expands.at[owner, pl.ds(2 * piece, 2)]
        device = next_of[way] if step == 1 else after_next[way]
        return remote(part, part, up_send.at[way, hop, piece, step - 1], up_recv.at[way, hop + step - 1, piece], device)

    def up_sends(way, hop, piece):
        if hop < EXPAND_LATE:
            steps = (1,)
        elif (hop - EXPAND_LATE) % 2 == 0:
            steps = (2, 1)
        else:
            steps = ()
        for step in steps:
            if hop + step < HALF or (hop + step == HALF and piece == way):
                yield up_copy(way, hop, owner_at(way, hop), piece, step)

    def up_forward(way, hop):
        for piece in (way, 1 - way):
            for copy in up_sends(way, hop, piece):
                copy.start()

    def upsib_copy(way, hop, which):
        shard = expands.at[owner_at(way, hop, which), up_part(way, hop)]
        return remote(shard, shard, upsib_send.at[way, hop], upsib_recv.at[way, hop], sibling)

    def up_hop(hop):
        for way in (0, 1):
            for piece in (way, 1 - way):
                if hop < HALF or piece == way:
                    up_copy(way, hop - 1, owner_at(way, hop), piece).wait_recv()
                    for copy in up_sends(way, hop, piece):
                        copy.start()
            upsib_copy(way, hop, core).start()

    for place in range(HELD):
        for way in (0, 1):
            chunk = ORDERS[way][place]
            ring_copy(way, 0, chunk, shrink_hbm.at[chunk]).start()

    loads[0].wait()
    loads[1].wait()

    def base_block(pair, carry):
        both = jnp.dot(act[...], kv[:, pl.ds(pl.multiple_of(pair * 2 * FEAT, 2 * FEAT), 2 * FEAT)], preferred_element_type=F32)
        part_out[2 * pair] = both[:, :FEAT].astype(BF16)
        part_out[2 * pair + 1] = both[:, FEAT:].astype(BF16)
        return carry

    lax.fori_loop(0, PEERS // 2, base_block, 0)

    def base_copy(index):
        offset = OFFSETS[index]
        other_x, other_y = peer(offset)
        return remote(
            part_out.at[other_x * YS + other_y], part_in.at[index], base_send.at[index], base_recv.at[index], peer_id(offset)
        )

    for index in range(len(OFFSETS)):
        base_copy(index).start()
    base[...] = jnp.dot(
        act[...], kv[:, pl.ds(pl.multiple_of(tensor * FEAT, FEAT), FEAT)], preferred_element_type=F32
    )

    for copy in loads[2:]:
        copy.wait()
    sib_copy(0, 0, core).start()
    slot_row = slots[...]
    named = jnp.zeros((1, REQ), jnp.int32)
    for slot in range(SLOTS):
        named = jnp.where(slot_row == slot, owners[slot] * HELD + locals_[slot], named)
    adapter[...] = jnp.broadcast_to(named, adapter.shape)
    act_t[...] = act[...].T
    slot_column = jnp.broadcast_to(slot_row, (FEAT, REQ)).T
    lane_slot = lax.broadcasted_iota(jnp.int32, (REQ, FEAT), 1) // RANK
    for pair in range(SLOTS // 2):
        hot[:, pair * FEAT : (pair + 1) * FEAT] = jnp.where(slot_column == lane_slot + 2 * pair, 1.0, 0.0).astype(BF16)
    picked[...] = jnp.zeros_like(picked)

    def shrink_with(owner, first=0, count=HELD):
        weights = shrinks[owner, pl.ds(first, count)].reshape(count * RANK, WIDTH)
        block = jnp.dot(weights, act_t[...], preferred_element_type=F32)
        total = picked[...]
        for local in range(count):
            hit = adapter[0:1, :] == owner * HELD + first + local
            total = jnp.where(hit, block[local * RANK : (local + 1) * RANK], total)
        picked[...] = total

    def add_base(index):
        base_copy(index).wait_recv()
        base[...] += part_in[index].astype(F32)

    def work(place, hop):
        way = place % 2
        if place < 2:
            shrink_with(owner_at(way, hop))
        elif way == 0:
            sib_copy(0, hop, 1 - core).wait_recv()
            shrink_with(owner_at(0, hop, 1 - core))
        else:
            @pl.when(hop > 0)
            def _():
                sib_copy(1, hop, 1 - core).wait_recv()

            shrink_with(owner_at(1, hop, 1 - core))

    def shrink_hop(hop, carry):
        for place in range(HELD):
            for way in (0, 1):
                chunk = ORDERS[way][place]
                ring_arrived(way, hop, chunk)
                if chunk in KEPT[way]:
                    ring_forward(way, hop, chunk)
                else:
                    pl.when(hop < HALF - 1)(functools.partial(ring_forward, way, hop, chunk))
            work(place, hop - 1)
        for way in (0, 1):
            sib_copy(way, hop, core).start()
        return carry

    lax.fori_loop(1, 5, shrink_hop, 0)
    up_forward(0, 0)
    up_forward(1, 0)
    upsib_copy(0, 0, core).start()
    for hop in range(5, HALF):
        shrink_hop(hop, 0)
        up_hop(hop - 4)
        for index in range(5 * (hop - 5), 5 * (hop - 4)):
            add_base(index)
    for place in range(HELD):
        work(place, HALF - 1)
    for way in (0, 1):
        for place in (0, 1):
            ring_arrived(way, HALF, ORDERS[way][place])
        sib_half(way, core).start()
    up_hop(EXPAND_LATE)
    for way in (0, 1):
        shrink_with(owner_at(way, HALF), 2 * way, 2)
    for way in (0, 1):
        sib_half(way, 1 - core).wait_recv()
        shrink_with(owner_at(way, HALF, 1 - core), 2 * way, 2)

    def piece_of(ref, at_x, at_y):
        return ref.at[pl.ds(pl.multiple_of(at_x * 16, 16), 16), pl.ds(pl.multiple_of(at_y * 128, 128), 128)]

    def sum_copy(index):
        other_x, other_y = peer(OFFSETS[index])
        return remote(
            piece_of(picked, other_x, other_y), sum_in.at[index], sum_send.at[index], sum_recv.at[index], peer_id(OFFSETS[index])
        )

    def all_copy(index, sign=1):
        at_x, at_y = (x, y) if sign == 1 else peer(OFFSETS[index], -1)
        return remote(
            piece_of(shrunk_t, at_x, at_y), piece_of(shrunk_t, at_x, at_y), all_send.at[index], all_recv.at[index],
            peer_id(OFFSETS[index]),
        )

    for index in range(len(OFFSETS)):
        sum_copy(index).start()
    up_hop(6)
    up_hop(5)
    total = piece_of(picked, x, y)[...]
    for index in reversed(range(len(OFFSETS))):
        sum_copy(index).wait_recv()
        total += sum_in[index]
    piece_of(shrunk_t, x, y)[...] = total.astype(BF16)
    for index in range(len(OFFSETS)):
        all_copy(index).start()
    for index in reversed(range(len(OFFSETS))):
        all_copy(index, -1).wait_recv()
    twice = jnp.concatenate([shrunk_t[...], shrunk_t[...]], axis=0).T
    for pair in range(SLOTS // 2):
        hot[:, pair * FEAT : (pair + 1) * FEAT] *= twice
    up_hop(7)
    up_hop(HALF)
    upsib_copy(0, 0, 1 - core).wait_recv()
    for hop in range(1, HALF + 1):
        for way in (0, 1):
            upsib_copy(way, hop, 1 - core).wait_recv()
    for slot in range(SLOTS):
        rows[slot * RANK : (slot + 1) * RANK, :] = expands[owners[slot], locals_[slot]]
    out[...] = (base[...] + jnp.dot(hot[...], rows[...], preferred_element_type=F32)).astype(BF16)

    for way in (0, 1):
        for hop in range(HALF):
            for chunk in range(HELD):
                if hop < HALF - 1 or chunk in KEPT[way]:
                    ring_copy(way, hop, chunk, shrinks.at[owner_at(way, hop), chunk]).wait_send()
            for piece in (0, 1):
                for copy in up_sends(way, hop, piece):
                    copy.wait_send()
        for hop in range(HALF + 1):
            if hop or way == 0:
                (sib_half(way, core) if hop == HALF else sib_copy(way, hop, core)).wait_send()
                upsib_copy(way, hop, core).wait_send()
    for index in range(len(OFFSETS)):
        base_copy(index).wait_send()
        sum_copy(index).wait_send()
        all_copy(index).wait_send()


def shards(activations, kv_weight, pool_shrink, pool_expand, request_slot, slot_owner, slot_local):
    peers = len(OFFSETS)
    dma = pltpu.SemaphoreType.DMA
    hbm = pl.BlockSpec(memory_space=pltpu.HBM)
    vmem = pl.BlockSpec(memory_space=pltpu.VMEM)
    return pl.pallas_call(
        kernel,
        out_shape=jax.ShapeDtypeStruct((REQ, FEAT), BF16),
        in_specs=[hbm] * 7,
        out_specs=vmem,
        scratch_shapes=[
            pltpu.SMEM((SLOTS,), jnp.int32),
            pltpu.SMEM((SLOTS,), jnp.int32),
            pltpu.VMEM((1, REQ), jnp.int32),
            pltpu.VMEM((REQ, WIDTH), BF16),
            pltpu.VMEM((WIDTH, REQ), BF16),
            pltpu.VMEM((WIDTH, PEERS * FEAT), BF16),
            pltpu.VMEM((OWNERS, HELD, RANK, WIDTH), BF16),
            pltpu.VMEM((OWNERS, HELD, RANK, FEAT), BF16),
            pltpu.VMEM((PEERS, REQ, FEAT), BF16),
            pltpu.VMEM((peers, REQ, FEAT), BF16),
            pltpu.VMEM((REQ, FEAT), F32),
            pltpu.VMEM((8, REQ), jnp.int32),
            pltpu.VMEM((RANK, REQ), F32),
            pltpu.VMEM((peers, 16, 128), F32),
            pltpu.VMEM((RANK, REQ), BF16),
            pltpu.VMEM((REQ, SLOTS * RANK), BF16),
            pltpu.VMEM((SLOTS * RANK, FEAT), BF16),
            dma((7,)),
            dma((2, HALF, HELD)),
            dma((2, HALF, HELD)),
            dma((2, HALF + 1)),
            dma((2, HALF + 1)),
            dma((2, HALF, 2, 2)),
            dma((2, HALF, 2)),
            dma((2, HALF + 1)),
            dma((2, HALF + 1)),
            dma((peers,)),
            dma((peers,)),
            dma((peers,)),
            dma((peers,)),
            dma((peers,)),
            dma((peers,)),
        ],
        compiler_params=pltpu.CompilerParams(
            collective_id=0, has_side_effects=True, vmem_limit_bytes=60 * 2**20
        ),
    )(
        slot_owner.reshape(-1), slot_local.reshape(-1), request_slot.reshape(1, -1),
        activations, kv_weight, pool_shrink, pool_expand,
    )


def solution(mesh):
    in_specs = (
        P("dp", "tensor"),
        P("tensor", None),
        P("dp", None, "tensor"),
        P("dp", None, "tensor"),
        P("dp"),
        P("dp", None),
        P("dp", None),
    )
    out_specs = P("dp", "tensor")
    return jax.shard_map(shards, mesh=mesh, in_specs=in_specs, out_specs=out_specs, check_vma=False)
```

```python
import functools

import jax
import jax.numpy as jnp
from jax import lax
from jax.experimental import pallas as pl
from jax.experimental.pallas import tpu as pltpu
from jax.sharding import PartitionSpec as P

MESH = pl.DeviceIdType.MESH
BF16, F32 = jnp.bfloat16, jnp.float32
PLANES, CORES, XS, YS = 16, 2, 4, 4
OWNERS, PEERS = PLANES * CORES, XS * YS
HELD, RANK, SLOTS = 4, 64, 32
REQ, WIDTH, FEAT = 512, 512, 128
HALF = PLANES // 2
ORDERS = ((0, 1, 2, 3), (2, 3, 0, 1))
KEPT = ((0, 1), (2, 3))
EXPAND_LATE = 4


def away(offset):
    return sum(min(step, 4 - step) for step in offset)


OFFSETS = sorted(((i, j) for i in range(XS) for j in range(YS) if i or j), key=lambda offset: -away(offset))


def remote(src, dst, send, recv, device):
    return pltpu.make_async_remote_copy(
        src_ref=src, dst_ref=dst, send_sem=send, recv_sem=recv, device_id=device, device_id_type=MESH
    )


def kernel(
    owners_hbm, locals_hbm, slots_hbm, act_hbm, kv_hbm, shrink_hbm, expand_hbm, out,
    owners, locals_, slots, act, act_t, kv, shrinks, expands, part_out, part_in, base, adapter, picked, sum_in, shrunk_t, hot, rows,
    load, ring_send, ring_recv, sib_send, sib_recv, up_send, up_recv, upsib_send, upsib_recv,
    base_send, base_recv, sum_send, sum_recv, all_send, all_recv,
):
    dp, tensor = lax.axis_index("dp"), lax.axis_index("tensor")
    z, core = dp // CORES, dp % CORES
    x, y = tensor // YS, tensor % YS

    def owner_at(way, hop, which=core):
        plane = (z - hop + PLANES) % PLANES if way == 0 else (z + hop) % PLANES
        return plane * CORES + which

    next_of = ({"dp": owner_at(1, 1)}, {"dp": owner_at(0, 1)})
    after_next = ({"dp": owner_at(1, 2)}, {"dp": owner_at(0, 2)})
    sibling = {"dp": z * CORES + 1 - core}

    def peer(offset, sign=1):
        other_x = (x + sign * offset[0] + XS) % XS
        other_y = (y + sign * offset[1] + YS) % YS
        return other_x, other_y

    def peer_id(offset, sign=1):
        other_x, other_y = peer(offset, sign)
        return {"tensor": other_x * YS + other_y}

    loads = [
        pltpu.make_async_copy(act_hbm, act, load.at[0]),
        pltpu.make_async_copy(kv_hbm, kv, load.at[1]),
        pltpu.make_async_copy(shrink_hbm, shrinks.at[dp], load.at[2]),
        pltpu.make_async_copy(expand_hbm, expands.at[dp], load.at[3]),
        pltpu.make_async_copy(owners_hbm, owners, load.at[4]),
        pltpu.make_async_copy(locals_hbm, locals_, load.at[5]),
        pltpu.make_async_copy(slots_hbm, slots, load.at[6]),
    ]
    barrier = pltpu.get_barrier_semaphore()
    for device in (*next_of, *after_next, sibling):
        pl.semaphore_signal(barrier, inc=1, device_id=device, device_id_type=MESH)
    for offset in OFFSETS:
        pl.semaphore_signal(barrier, inc=1, device_id=peer_id(offset), device_id_type=MESH)
    for copy in loads:
        copy.start()
    pl.semaphore_wait(barrier, 5 + len(OFFSETS))

    def ring_copy(way, hop, chunk, src):
        return remote(
            src, shrinks.at[owner_at(way, hop), chunk], ring_send.at[way, hop, chunk],
            ring_recv.at[way, hop, chunk], next_of[way],
        )

    def ring_forward(way, hop, chunk):
        ring_copy(way, hop, chunk, shrinks.at[owner_at(way, hop), chunk]).start()

    def ring_arrived(way, hop, chunk):
        owner = owner_at(way, hop)
        remote(
            shrinks.at[owner, chunk], shrinks.at[owner, chunk], ring_send.at[way, hop, chunk],
            ring_recv.at[way, hop - 1, chunk], next_of[way],
        ).wait_recv()

    def sib_copy(way, hop, which):
        shard = shrinks.at[owner_at(way, hop, which)]
        return remote(shard, shard, sib_send.at[way, hop], sib_recv.at[way, hop], sibling)

    def sib_half(way, which):
        shard = shrinks.at[owner_at(way, HALF, which), pl.ds(2 * way, 2)]
        return remote(shard, shard, sib_send.at[way, HALF], sib_recv.at[way, HALF], sibling)

    def up_part(way, hop):
        return pl.ds(2 * way, 2) if hop == HALF else pl.ds(0, HELD)

    def up_copy(way, hop, owner, piece, step=1):
        part = expands.at[owner, pl.ds(2 * piece, 2)]
        device = next_of[way] if step == 1 else after_next[way]
        return remote(part, part, up_send.at[way, hop, piece, step - 1], up_recv.at[way, hop + step - 1, piece], device)

    def up_sends(way, hop, piece):
        if hop < EXPAND_LATE:
            steps = (1,)
        elif (hop - EXPAND_LATE) % 2 == 0:
            steps = (2, 1)
        else:
            steps = ()
        for step in steps:
            if hop + step < HALF or (hop + step == HALF and piece == way):
                yield up_copy(way, hop, owner_at(way, hop), piece, step)

    def up_forward(way, hop):
        for piece in (way, 1 - way):
            for copy in up_sends(way, hop, piece):
                copy.start()

    def upsib_copy(way, hop, which):
        shard = expands.at[owner_at(way, hop, which), up_part(way, hop)]
        return remote(shard, shard, upsib_send.at[way, hop], upsib_recv.at[way, hop], sibling)

    def up_arrived(hop, turn):
        for way in (0, 1):
            piece = way if turn == 0 else 1 - way
            if hop < HALF or turn == 0:
                up_copy(way, hop - 1, owner_at(way, hop), piece).wait_recv()
                for copy in up_sends(way, hop, piece):
                    copy.start()

    def up_shared(hop):
        for way in (0, 1):
            upsib_copy(way, hop, core).start()

    def up_hop(hop):
        for turn in (0, 1):
            up_arrived(hop, turn)
        up_shared(hop)

    for place in range(HELD):
        for way in (0, 1):
            chunk = ORDERS[way][place]
            ring_copy(way, 0, chunk, shrink_hbm.at[chunk]).start()

    def base_block(pair):
        both = jnp.dot(act[...], kv[:, pl.ds(pl.multiple_of(pair * 2 * FEAT, 2 * FEAT), 2 * FEAT)], preferred_element_type=F32)
        part_out[2 * pair] = both[:, :FEAT].astype(BF16)
        part_out[2 * pair + 1] = both[:, FEAT:].astype(BF16)

    def base_blocks(place):
        if place == 0:
            loads[0].wait()
            loads[1].wait()
        half = PEERS // 4
        lax.fori_loop(place * half, place * half + half, lambda pair, carry: (base_block(pair), carry)[1], 0)

    def base_copy(index):
        offset = OFFSETS[index]
        other_x, other_y = peer(offset)
        return remote(
            part_out.at[other_x * YS + other_y], part_in.at[index], base_send.at[index], base_recv.at[index], peer_id(offset)
        )

    def own_base():
        base[...] = jnp.dot(
            act[...], kv[:, pl.ds(pl.multiple_of(tensor * FEAT, FEAT), FEAT)], preferred_element_type=F32
        )

    def adapters():
        for copy in loads[2:]:
            copy.wait()
        slot_row = slots[...]
        named = jnp.zeros((1, REQ), jnp.int32)
        for slot in range(SLOTS):
            named = jnp.where(slot_row == slot, owners[slot] * HELD + locals_[slot], named)
        adapter[...] = jnp.broadcast_to(named, adapter.shape)
        act_t[...] = act[...].T
        picked[...] = jnp.zeros_like(picked)

    def hot_slots(place):
        slot_column = jnp.broadcast_to(slots[...], (FEAT, REQ)).T
        lane_slot = lax.broadcasted_iota(jnp.int32, (REQ, FEAT), 1) // RANK
        for pair in range(4 * place, 4 * place + 4):
            hot[:, pair * FEAT : (pair + 1) * FEAT] = jnp.where(slot_column == lane_slot + 2 * pair, 1.0, 0.0).astype(BF16)

    def first_work(place):
        if place < 2:
            base_blocks(place)
        elif place == 2:
            for index in range(len(OFFSETS)):
                base_copy(index).start()
            own_base()
        else:
            adapters()
            sib_copy(0, 0, core).start()

    def shrink_with(owner, first=0, count=HELD):
        weights = shrinks[owner, pl.ds(first, count)].reshape(count * RANK, WIDTH)
        block = jnp.dot(weights, act_t[...], preferred_element_type=F32)
        total = picked[...]
        for local in range(count):
            hit = adapter[0:1, :] == owner * HELD + first + local
            total = jnp.where(hit, block[local * RANK : (local + 1) * RANK], total)
        picked[...] = total

    def add_base(index):
        base_copy(index).wait_recv()
        base[...] += part_in[index].astype(F32)

    def work(place, hop):
        way = place % 2
        if place < 2:
            shrink_with(owner_at(way, hop))
        elif way == 0:
            sib_copy(0, hop, 1 - core).wait_recv()
            shrink_with(owner_at(0, hop, 1 - core))
        else:
            sib_copy(1, hop, 1 - core).wait_recv()
            shrink_with(owner_at(1, hop, 1 - core))

    def own_work(place):
        if place == 0:
            shrink_with(dp)
        elif place == 1:
            sib_copy(0, 0, 1 - core).wait_recv()
            shrink_with(sibling["dp"])

    def early(place, hop):
        pl.when(hop == 1)(functools.partial(first_work, place))
        pl.when(hop == 2)(functools.partial(own_work, place))
        pl.when(hop == 3)(functools.partial(hot_slots, place))
        pl.when(hop > 1)(functools.partial(work, place, hop - 1))

    def late(place, hop):
        work(place, hop - 1)

    def shrink_hop(extra, hop, carry):
        for place in range(HELD):
            for way in (0, 1):
                chunk = ORDERS[way][place]
                ring_arrived(way, hop, chunk)
                if chunk in KEPT[way]:
                    ring_forward(way, hop, chunk)
                else:
                    pl.when(hop < HALF - 1)(functools.partial(ring_forward, way, hop, chunk))
            extra(place, hop)
        for way in (0, 1):
            sib_copy(way, hop, core).start()
        return carry

    lax.fori_loop(1, 5, functools.partial(shrink_hop, early), 0)
    up_forward(0, 0)
    up_forward(1, 0)
    upsib_copy(0, 0, core).start()
    for hop in range(5, HALF):
        shrink_hop(late, hop, 0)
        up_hop(hop - 4)
        for index in range(5 * (hop - 5), 5 * (hop - 4)):
            add_base(index)
    for place in range(HELD):
        work(place, HALF - 1)
    for way in (0, 1):
        for place in (0, 1):
            ring_arrived(way, HALF, ORDERS[way][place])
        sib_half(way, core).start()
    up_hop(EXPAND_LATE)
    for way in (0, 1):
        shrink_with(owner_at(way, HALF), 2 * way, 2)
    for way in (0, 1):
        sib_half(way, 1 - core).wait_recv()
        shrink_with(owner_at(way, HALF, 1 - core), 2 * way, 2)

    def piece_of(ref, at_x, at_y):
        return ref.at[pl.ds(pl.multiple_of(at_x * 16, 16), 16), pl.ds(pl.multiple_of(at_y * 128, 128), 128)]

    def sum_copy(index):
        other_x, other_y = peer(OFFSETS[index])
        return remote(
            piece_of(picked, other_x, other_y), sum_in.at[index], sum_send.at[index], sum_recv.at[index], peer_id(OFFSETS[index])
        )

    def all_copy(index, sign=1):
        at_x, at_y = (x, y) if sign == 1 else peer(OFFSETS[index], -1)
        return remote(
            piece_of(shrunk_t, at_x, at_y), piece_of(shrunk_t, at_x, at_y), all_send.at[index], all_recv.at[index],
            peer_id(OFFSETS[index]),
        )

    for index in range(len(OFFSETS)):
        sum_copy(index).start()
    up_arrived(6, 0)
    total = piece_of(picked, x, y)[...]
    for index in reversed(range(len(OFFSETS))):
        sum_copy(index).wait_recv()
        total += sum_in[index]
    piece_of(shrunk_t, x, y)[...] = total.astype(BF16)
    for index in range(len(OFFSETS)):
        all_copy(index).start()
    up_arrived(6, 1)
    up_shared(6)
    up_hop(5)
    for index in range(len(OFFSETS)):
        base_copy(index).wait_send()
        sum_copy(index).wait_send()
    for way in (0, 1):
        for hop in range(HALF):
            for chunk in range(HELD):
                if hop < HALF - 1 or chunk in KEPT[way]:
                    ring_copy(way, hop, chunk, shrinks.at[owner_at(way, hop), chunk]).wait_send()
            for piece in (0, 1):
                if hop < 6:
                    for copy in up_sends(way, hop, piece):
                        copy.wait_send()
        for hop in range(HALF + 1):
            if hop or way == 0:
                (sib_half(way, core) if hop == HALF else sib_copy(way, hop, core)).wait_send()
                if hop < 5:
                    upsib_copy(way, hop, core).wait_send()
    up_hop(7)
    up_hop(HALF)
    for index in reversed(range(len(OFFSETS))):
        all_copy(index, -1).wait_recv()
    for index in range(len(OFFSETS)):
        all_copy(index).wait_send()
    twice = jnp.concatenate([shrunk_t[...], shrunk_t[...]], axis=0).T
    for pair in range(SLOTS // 2):
        hot[:, pair * FEAT : (pair + 1) * FEAT] *= twice
    upsib_copy(0, 0, 1 - core).wait_recv()
    for hop in range(1, HALF + 1):
        for way in (0, 1):
            upsib_copy(way, hop, 1 - core).wait_recv()
    for slot in range(SLOTS):
        rows[slot * RANK : (slot + 1) * RANK, :] = expands[owners[slot], locals_[slot]]
    out[...] = (base[...] + jnp.dot(hot[...], rows[...], preferred_element_type=F32)).astype(BF16)

    for way in (0, 1):
        for piece in (0, 1):
            for copy in up_sends(way, 6, piece):
                copy.wait_send()
        for hop in range(5, HALF + 1):
            upsib_copy(way, hop, core).wait_send()


def shards(activations, kv_weight, pool_shrink, pool_expand, request_slot, slot_owner, slot_local):
    peers = len(OFFSETS)
    dma = pltpu.SemaphoreType.DMA
    hbm = pl.BlockSpec(memory_space=pltpu.HBM)
    vmem = pl.BlockSpec(memory_space=pltpu.VMEM)
    return pl.pallas_call(
        kernel,
        out_shape=jax.ShapeDtypeStruct((REQ, FEAT), BF16),
        in_specs=[hbm] * 7,
        out_specs=vmem,
        scratch_shapes=[
            pltpu.SMEM((SLOTS,), jnp.int32),
            pltpu.SMEM((SLOTS,), jnp.int32),
            pltpu.VMEM((1, REQ), jnp.int32),
            pltpu.VMEM((REQ, WIDTH), BF16),
            pltpu.VMEM((WIDTH, REQ), BF16),
            pltpu.VMEM((WIDTH, PEERS * FEAT), BF16),
            pltpu.VMEM((OWNERS, HELD, RANK, WIDTH), BF16),
            pltpu.VMEM((OWNERS, HELD, RANK, FEAT), BF16),
            pltpu.VMEM((PEERS, REQ, FEAT), BF16),
            pltpu.VMEM((peers, REQ, FEAT), BF16),
            pltpu.VMEM((REQ, FEAT), F32),
            pltpu.VMEM((8, REQ), jnp.int32),
            pltpu.VMEM((RANK, REQ), F32),
            pltpu.VMEM((peers, 16, 128), F32),
            pltpu.VMEM((RANK, REQ), BF16),
            pltpu.VMEM((REQ, SLOTS * RANK), BF16),
            pltpu.VMEM((SLOTS * RANK, FEAT), BF16),
            dma((7,)),
            dma((2, HALF, HELD)),
            dma((2, HALF, HELD)),
            dma((2, HALF + 1)),
            dma((2, HALF + 1)),
            dma((2, HALF, 2, 2)),
            dma((2, HALF, 2)),
            dma((2, HALF + 1)),
            dma((2, HALF + 1)),
            dma((peers,)),
            dma((peers,)),
            dma((peers,)),
            dma((peers,)),
            dma((peers,)),
            dma((peers,)),
        ],
        compiler_params=pltpu.CompilerParams(
            collective_id=0, has_side_effects=True, vmem_limit_bytes=60 * 2**20
        ),
    )(
        slot_owner.reshape(-1), slot_local.reshape(-1), request_slot.reshape(1, -1),
        activations, kv_weight, pool_shrink, pool_expand,
    )


def solution(mesh):
    in_specs = (
        P("dp", "tensor"),
        P("tensor", None),
        P("dp", None, "tensor"),
        P("dp", None, "tensor"),
        P("dp"),
        P("dp", None),
        P("dp", None),
    )
    out_specs = P("dp", "tensor")
    return jax.shard_map(shards, mesh=mesh, in_specs=in_specs, out_specs=out_specs, check_vma=False)
```

```python
import functools

import jax
import jax.numpy as jnp
from jax import lax
from jax.experimental import pallas as pl
from jax.experimental.pallas import tpu as pltpu
from jax.sharding import PartitionSpec as P

MESH = pl.DeviceIdType.MESH
BF16, F32 = jnp.bfloat16, jnp.float32
PLANES, CORES, XS, YS = 16, 2, 4, 4
OWNERS, PEERS = PLANES * CORES, XS * YS
HELD, RANK, SLOTS = 4, 64, 32
REQ, WIDTH, FEAT = 512, 512, 128
HALF = PLANES // 2
ORDERS = ((0, 1, 2, 3), (2, 3, 0, 1))
KEPT = ((0, 1), (2, 3))
EXPAND_LATE = 4


def away(offset):
    return sum(min(step, 4 - step) for step in offset)


OFFSETS = sorted(((i, j) for i in range(XS) for j in range(YS) if i or j), key=lambda offset: -away(offset))


def remote(src, dst, send, recv, device):
    return pltpu.make_async_remote_copy(
        src_ref=src, dst_ref=dst, send_sem=send, recv_sem=recv, device_id=device, device_id_type=MESH
    )


def kernel(
    owners_hbm, locals_hbm, slots_hbm, act_hbm, kv_hbm, shrink_hbm, expand_hbm, out,
    owners, locals_, slots, act, act_t, kv, shrinks, expands, part_out, part_in, base, adapter, picked, sum_in, shrunk_t, hot, rows,
    load, ring_send, ring_recv, sib_send, sib_recv, up_send, up_recv, upsib_send, upsib_recv,
    base_send, base_recv, sum_send, sum_recv, all_send, all_recv,
):
    dp, tensor = lax.axis_index("dp"), lax.axis_index("tensor")
    z, core = dp // CORES, dp % CORES
    x, y = tensor // YS, tensor % YS

    def owner_at(way, hop, which=core):
        plane = (z - hop + PLANES) % PLANES if way == 0 else (z + hop) % PLANES
        return plane * CORES + which

    next_of = ({"dp": owner_at(1, 1)}, {"dp": owner_at(0, 1)})
    after_next = ({"dp": owner_at(1, 2)}, {"dp": owner_at(0, 2)})
    sibling = {"dp": z * CORES + 1 - core}

    def in_bytes(ref, semaphore):
        return remote(ref, ref, semaphore, semaphore, sibling)

    all_pieces = rows.at[pl.ds(0, 16 * len(OFFSETS))]

    def peer(offset, sign=1):
        other_x = (x + sign * offset[0] + XS) % XS
        other_y = (y + sign * offset[1] + YS) % YS
        return other_x, other_y

    def peer_id(offset, sign=1):
        other_x, other_y = peer(offset, sign)
        return {"tensor": other_x * YS + other_y}

    loads = [
        pltpu.make_async_copy(act_hbm, act, load.at[0]),
        pltpu.make_async_copy(kv_hbm, kv, load.at[1]),
        pltpu.make_async_copy(shrink_hbm, shrinks.at[dp], load.at[2]),
        pltpu.make_async_copy(expand_hbm, expands.at[dp], load.at[3]),
        pltpu.make_async_copy(owners_hbm, owners, load.at[4]),
        pltpu.make_async_copy(locals_hbm, locals_, load.at[5]),
        pltpu.make_async_copy(slots_hbm, slots, load.at[6]),
    ]
    barrier = pltpu.get_barrier_semaphore()
    for device in (*next_of, *after_next, sibling):
        pl.semaphore_signal(barrier, inc=1, device_id=device, device_id_type=MESH)
    for offset in OFFSETS:
        pl.semaphore_signal(barrier, inc=1, device_id=peer_id(offset), device_id_type=MESH)
    for copy in loads:
        copy.start()
    pl.semaphore_wait(barrier, 5 + len(OFFSETS))

    def ring_copy(way, hop, chunk, src):
        return remote(
            src, shrinks.at[owner_at(way, hop), chunk], ring_send.at[0],
            ring_recv.at[way, hop, chunk], next_of[way],
        )

    def ring_forward(way, hop, chunk):
        ring_copy(way, hop, chunk, shrinks.at[owner_at(way, hop), chunk]).start()

    def ring_arrived(way, hop, chunk):
        owner = owner_at(way, hop)
        remote(
            shrinks.at[owner, chunk], shrinks.at[owner, chunk], ring_send.at[0],
            ring_recv.at[way, hop - 1, chunk], next_of[way],
        ).wait_recv()

    def sib_copy(way, hop, which):
        shard = shrinks.at[owner_at(way, hop, which)]
        return remote(shard, shard, sib_send.at[0], sib_recv.at[way, hop], sibling)

    def sib_half(way, which):
        shard = shrinks.at[owner_at(way, HALF, which), pl.ds(2 * way, 2)]
        return remote(shard, shard, sib_send.at[0], sib_recv.at[way, HALF], sibling)

    def up_part(way, hop):
        return pl.ds(2 * way, 2) if hop == HALF else pl.ds(0, HELD)

    def up_copy(way, hop, owner, piece, step=1):
        part = expands.at[owner, pl.ds(2 * piece, 2)]
        device = next_of[way] if step == 1 else after_next[way]
        return remote(part, part, up_send.at[0], up_recv.at[way, hop + step - 1, piece], device)

    def up_sends(way, hop, piece):
        if hop < EXPAND_LATE:
            steps = (1,)
        elif (hop - EXPAND_LATE) % 2 == 0:
            steps = (2, 1)
        else:
            steps = ()
        for step in steps:
            if hop + step < HALF or (hop + step == HALF and piece == way):
                yield up_copy(way, hop, owner_at(way, hop), piece, step)

    def up_forward(way, hop):
        for piece in (way, 1 - way):
            for copy in up_sends(way, hop, piece):
                copy.start()

    def upsib_copy(way, hop, which):
        shard = expands.at[owner_at(way, hop, which), up_part(way, hop)]
        return remote(shard, shard, upsib_send.at[0], upsib_recv.at[0], sibling)

    def up_arrived(hop, turn):
        for way in (0, 1):
            piece = way if turn == 0 else 1 - way
            if hop < HALF or turn == 0:
                up_copy(way, hop - 1, owner_at(way, hop), piece).wait_recv()
                for copy in up_sends(way, hop, piece):
                    copy.start()

    def up_shared(hop):
        for way in (0, 1):
            upsib_copy(way, hop, core).start()

    def up_hop(hop):
        for turn in (0, 1):
            up_arrived(hop, turn)
        up_shared(hop)

    for place in range(HELD):
        for way in (0, 1):
            chunk = ORDERS[way][place]
            ring_copy(way, 0, chunk, shrink_hbm.at[chunk]).start()

    def base_block(pair):
        both = jnp.dot(act[...], kv[:, pl.ds(pl.multiple_of(pair * 2 * FEAT, 2 * FEAT), 2 * FEAT)], preferred_element_type=F32)
        part_out[2 * pair] = both[:, :FEAT].astype(BF16)
        part_out[2 * pair + 1] = both[:, FEAT:].astype(BF16)

    def base_blocks(place):
        if place == 0:
            loads[0].wait()
            loads[1].wait()
        half = PEERS // 4
        lax.fori_loop(place * half, place * half + half, lambda pair, carry: (base_block(pair), carry)[1], 0)

    def base_copy(index):
        offset = OFFSETS[index]
        other_x, other_y = peer(offset)
        return remote(
            part_out.at[other_x * YS + other_y], part_in.at[index], base_send.at[0], base_recv.at[index // 5], peer_id(offset)
        )

    def own_base():
        base[...] = jnp.dot(
            act[...], kv[:, pl.ds(pl.multiple_of(tensor * FEAT, FEAT), FEAT)], preferred_element_type=F32
        )

    def adapters():
        for copy in loads[2:]:
            copy.wait()
        slot_row = slots[...]
        named = jnp.zeros((1, REQ), jnp.int32)
        for slot in range(SLOTS):
            named = jnp.where(slot_row == slot, owners[slot] * HELD + locals_[slot], named)
        adapter[...] = jnp.broadcast_to(named, adapter.shape)
        act_t[...] = act[...].T
        picked[...] = jnp.zeros_like(picked)

    def hot_slots(place):
        slot_column = jnp.broadcast_to(slots[...], (FEAT, REQ)).T
        lane_slot = lax.broadcasted_iota(jnp.int32, (REQ, FEAT), 1) // RANK
        for pair in range(4 * place, 4 * place + 4):
            hot[:, pair * FEAT : (pair + 1) * FEAT] = jnp.where(slot_column == lane_slot + 2 * pair, 1.0, 0.0).astype(BF16)

    def first_work(place):
        if place < 2:
            base_blocks(place)
        elif place == 2:
            for index in range(len(OFFSETS)):
                base_copy(index).start()
            own_base()
        else:
            adapters()
            sib_copy(0, 0, core).start()

    def shrink_with(owner, first=0, count=HELD):
        weights = shrinks[owner, pl.ds(first, count)].reshape(count * RANK, WIDTH)
        block = jnp.dot(weights, act_t[...], preferred_element_type=F32)
        total = picked[...]
        for local in range(count):
            hit = adapter[0:1, :] == owner * HELD + first + local
            total = jnp.where(hit, block[local * RANK : (local + 1) * RANK], total)
        picked[...] = total

    def add_base(index):
        if index % 5 == 0:
            in_bytes(part_in.at[pl.ds(index, 5)], base_recv.at[index // 5]).wait_recv()
        base[...] += part_in[index].astype(F32)

    def work(place, hop):
        way = place % 2
        if place < 2:
            shrink_with(owner_at(way, hop))
        elif way == 0:
            sib_copy(0, hop, 1 - core).wait_recv()
            shrink_with(owner_at(0, hop, 1 - core))
        else:
            sib_copy(1, hop, 1 - core).wait_recv()
            shrink_with(owner_at(1, hop, 1 - core))

    def own_work(place):
        if place == 0:
            shrink_with(dp)
        elif place == 1:
            sib_copy(0, 0, 1 - core).wait_recv()
            shrink_with(sibling["dp"])

    def early(place, hop):
        pl.when(hop == 1)(functools.partial(first_work, place))
        pl.when(hop == 2)(functools.partial(own_work, place))
        pl.when(hop == 3)(functools.partial(hot_slots, place))
        pl.when(hop > 1)(functools.partial(work, place, hop - 1))

    def late(place, hop):
        work(place, hop - 1)

    def shrink_hop(extra, hop, carry):
        for place in range(HELD):
            for way in (0, 1):
                chunk = ORDERS[way][place]
                ring_arrived(way, hop, chunk)
                if chunk in KEPT[way]:
                    ring_forward(way, hop, chunk)
                else:
                    pl.when(hop < HALF - 1)(functools.partial(ring_forward, way, hop, chunk))
            extra(place, hop)
        for way in (0, 1):
            sib_copy(way, hop, core).start()
        return carry

    lax.fori_loop(1, 5, functools.partial(shrink_hop, early), 0)
    up_forward(0, 0)
    up_forward(1, 0)
    upsib_copy(0, 0, core).start()
    for hop in range(5, HALF):
        shrink_hop(late, hop, 0)
        up_hop(hop - 4)
        for index in range(5 * (hop - 5), 5 * (hop - 4)):
            add_base(index)
    for place in range(HELD):
        work(place, HALF - 1)
    for way in (0, 1):
        for place in (0, 1):
            ring_arrived(way, HALF, ORDERS[way][place])
        sib_half(way, core).start()
    up_hop(EXPAND_LATE)
    for way in (0, 1):
        shrink_with(owner_at(way, HALF), 2 * way, 2)
    for way in (0, 1):
        sib_half(way, 1 - core).wait_recv()
        shrink_with(owner_at(way, HALF, 1 - core), 2 * way, 2)

    def piece_of(ref, at_x, at_y):
        return ref.at[pl.ds(pl.multiple_of(at_x * 16, 16), 16), pl.ds(pl.multiple_of(at_y * 128, 128), 128)]

    def sum_copy(index):
        other_x, other_y = peer(OFFSETS[index])
        return remote(
            piece_of(picked, other_x, other_y), sum_in.at[index], sum_send.at[0], sum_recv.at[0], peer_id(OFFSETS[index])
        )

    def all_copy(index):
        return remote(
            piece_of(shrunk_t, x, y), piece_of(shrunk_t, x, y), all_send.at[0], all_recv.at[0],
            peer_id(OFFSETS[index]),
        )

    for index in range(len(OFFSETS)):
        sum_copy(index).start()
    up_arrived(6, 0)
    total = piece_of(picked, x, y)[...]
    in_bytes(sum_in, sum_recv.at[0]).wait_recv()
    for index in range(len(OFFSETS)):
        total += sum_in[index]
    piece_of(shrunk_t, x, y)[...] = total.astype(BF16)
    for index in range(len(OFFSETS)):
        all_copy(index).start()
    up_arrived(6, 1)
    up_shared(6)
    up_hop(5)
    up_hop(7)
    up_hop(HALF)
    in_bytes(all_pieces, all_recv.at[0]).wait_recv()
    twice = jnp.concatenate([shrunk_t[...], shrunk_t[...]], axis=0).T
    for pair in range(SLOTS // 2):
        hot[:, pair * FEAT : (pair + 1) * FEAT] *= twice
    in_bytes(expands.at[pl.ds(0, PLANES)], upsib_recv.at[0]).wait_recv()
    for slot in range(SLOTS):
        rows[slot * RANK : (slot + 1) * RANK, :] = expands[owners[slot], locals_[slot]]
    out[...] = (base[...] + jnp.dot(hot[...], rows[...], preferred_element_type=F32)).astype(BF16)

    chunks = 2 * ((HALF - 1) * HELD + 2)
    in_bytes(shrinks.at[pl.ds(0, chunks // HELD)], ring_send.at[0]).wait_send()
    in_bytes(shrinks.at[pl.ds(0, PLANES)], sib_send.at[0]).wait_send()
    in_bytes(expands.at[pl.ds(0, PLANES - 1)], up_send.at[0]).wait_send()
    in_bytes(expands.at[pl.ds(0, PLANES)], upsib_send.at[0]).wait_send()
    in_bytes(part_in, base_send.at[0]).wait_send()
    in_bytes(sum_in, sum_send.at[0]).wait_send()
    in_bytes(all_pieces, all_send.at[0]).wait_send()


def shards(activations, kv_weight, pool_shrink, pool_expand, request_slot, slot_owner, slot_local):
    peers = len(OFFSETS)
    dma = pltpu.SemaphoreType.DMA
    hbm = pl.BlockSpec(memory_space=pltpu.HBM)
    vmem = pl.BlockSpec(memory_space=pltpu.VMEM)
    return pl.pallas_call(
        kernel,
        out_shape=jax.ShapeDtypeStruct((REQ, FEAT), BF16),
        in_specs=[hbm] * 7,
        out_specs=vmem,
        scratch_shapes=[
            pltpu.SMEM((SLOTS,), jnp.int32),
            pltpu.SMEM((SLOTS,), jnp.int32),
            pltpu.VMEM((1, REQ), jnp.int32),
            pltpu.VMEM((REQ, WIDTH), BF16),
            pltpu.VMEM((WIDTH, REQ), BF16),
            pltpu.VMEM((WIDTH, PEERS * FEAT), BF16),
            pltpu.VMEM((OWNERS, HELD, RANK, WIDTH), BF16),
            pltpu.VMEM((OWNERS, HELD, RANK, FEAT), BF16),
            pltpu.VMEM((PEERS, REQ, FEAT), BF16),
            pltpu.VMEM((peers, REQ, FEAT), BF16),
            pltpu.VMEM((REQ, FEAT), F32),
            pltpu.VMEM((8, REQ), jnp.int32),
            pltpu.VMEM((RANK, REQ), F32),
            pltpu.VMEM((peers, 16, 128), F32),
            pltpu.VMEM((RANK, REQ), BF16),
            pltpu.VMEM((REQ, SLOTS * RANK), BF16),
            pltpu.VMEM((SLOTS * RANK, FEAT), BF16),
            dma((7,)),
            dma((1,)),
            dma((2, HALF, HELD)),
            dma((1,)),
            dma((2, HALF + 1)),
            dma((1,)),
            dma((2, HALF, 2)),
            dma((1,)),
            dma((1,)),
            dma((1,)),
            dma((3,)),
            dma((1,)),
            dma((1,)),
            dma((1,)),
            dma((1,)),
        ],
        compiler_params=pltpu.CompilerParams(
            collective_id=0, has_side_effects=True, vmem_limit_bytes=60 * 2**20
        ),
    )(
        slot_owner.reshape(-1), slot_local.reshape(-1), request_slot.reshape(1, -1),
        activations, kv_weight, pool_shrink, pool_expand,
    )


def solution(mesh):
    in_specs = (
        P("dp", "tensor"),
        P("tensor", None),
        P("dp", None, "tensor"),
        P("dp", None, "tensor"),
        P("dp"),
        P("dp", None),
        P("dp", None),
    )
    out_specs = P("dp", "tensor")
    return jax.shard_map(shards, mesh=mesh, in_specs=in_specs, out_specs=out_specs, check_vma=False)
```

```python
import functools

import jax
import jax.numpy as jnp
from jax import lax
from jax.experimental import pallas as pl
from jax.experimental.pallas import tpu as pltpu
from jax.sharding import PartitionSpec as P

MESH = pl.DeviceIdType.MESH
BF16, F32 = jnp.bfloat16, jnp.float32
PLANES, CORES, XS, YS = 16, 2, 4, 4
OWNERS, PEERS = PLANES * CORES, XS * YS
HELD, RANK, SLOTS = 4, 64, 32
REQ, WIDTH, FEAT = 512, 512, 128
HALF = PLANES // 2
EXPAND_LATE = 4


def away(offset):
    return sum(min(step, 4 - step) for step in offset)


OFFSETS = sorted(((i, j) for i in range(XS) for j in range(YS) if i or j), key=lambda offset: -away(offset))


def remote(src, dst, send, recv, device):
    return pltpu.make_async_remote_copy(
        src_ref=src, dst_ref=dst, send_sem=send, recv_sem=recv, device_id=device, device_id_type=MESH
    )


def kernel(
    owners_hbm, locals_hbm, slots_hbm, act_hbm, kv_hbm, shrink_hbm, expand_hbm, out,
    owners, locals_, slots, act, act_t, kv, shrinks, expands, part_out, part_in, base, adapter, picked, sum_in, shrunk_t, hot, rows,
    load, ring_send, ring_recv, sib_send, sib_recv, up_send, up_recv, upsib_send, upsib_recv,
    base_send, base_recv, sum_send, sum_recv, all_send, all_recv,
):
    dp, tensor = lax.axis_index("dp"), lax.axis_index("tensor")
    z, core = dp // CORES, dp % CORES
    x, y = tensor // YS, tensor % YS

    def owner_at(way, hop, which=core):
        plane = (z - hop + PLANES) % PLANES if way == 0 else (z + hop) % PLANES
        return plane * CORES + which

    next_of = ({"dp": owner_at(1, 1)}, {"dp": owner_at(0, 1)})
    after_next = ({"dp": owner_at(1, 2)}, {"dp": owner_at(0, 2)})
    sibling = {"dp": z * CORES + 1 - core}

    def in_bytes(ref, semaphore):
        return remote(ref, ref, semaphore, semaphore, sibling)

    all_pieces = rows.at[pl.ds(0, 16 * len(OFFSETS))]

    def peer(offset, sign=1):
        other_x = (x + sign * offset[0] + XS) % XS
        other_y = (y + sign * offset[1] + YS) % YS
        return other_x, other_y

    def peer_id(offset, sign=1):
        other_x, other_y = peer(offset, sign)
        return {"tensor": other_x * YS + other_y}

    loads = [
        pltpu.make_async_copy(act_hbm, act, load.at[0]),
        pltpu.make_async_copy(kv_hbm, kv, load.at[1]),
        pltpu.make_async_copy(shrink_hbm, shrinks.at[dp], load.at[2]),
        pltpu.make_async_copy(expand_hbm, expands.at[dp], load.at[3]),
        pltpu.make_async_copy(owners_hbm, owners, load.at[4]),
        pltpu.make_async_copy(locals_hbm, locals_, load.at[5]),
        pltpu.make_async_copy(slots_hbm, slots, load.at[6]),
    ]
    barrier = pltpu.get_barrier_semaphore()
    for device in (*next_of, *after_next, sibling):
        pl.semaphore_signal(barrier, inc=1, device_id=device, device_id_type=MESH)
    for offset in OFFSETS:
        pl.semaphore_signal(barrier, inc=1, device_id=peer_id(offset), device_id_type=MESH)
    for copy in loads:
        copy.start()
    pl.semaphore_wait(barrier, 5 + len(OFFSETS))

    def ring_copy(way, hop, piece, src):
        return remote(
            src, shrinks.at[owner_at(way, hop), pl.ds(2 * piece, 2)], ring_send.at[0],
            ring_recv.at[way, hop, piece], next_of[way],
        )

    def ring_forward(way, hop, piece):
        ring_copy(way, hop, piece, shrinks.at[owner_at(way, hop), pl.ds(2 * piece, 2)]).start()

    def ring_arrived(way, hop, piece):
        part = shrinks.at[owner_at(way, hop), pl.ds(2 * piece, 2)]
        remote(part, part, ring_send.at[0], ring_recv.at[way, hop - 1, piece], next_of[way]).wait_recv()

    def sib_copy(way, hop, which):
        shard = shrinks.at[owner_at(way, hop, which)]
        return remote(shard, shard, sib_send.at[0], sib_recv.at[way, hop], sibling)

    def sib_half(way, which):
        shard = shrinks.at[owner_at(way, HALF, which), pl.ds(2 * way, 2)]
        return remote(shard, shard, sib_send.at[0], sib_recv.at[way, HALF], sibling)

    def up_part(way, hop):
        return pl.ds(2 * way, 2) if hop == HALF else pl.ds(0, HELD)

    def up_copy(way, hop, owner, piece, step=1):
        part = expands.at[owner, pl.ds(2 * piece, 2)]
        device = next_of[way] if step == 1 else after_next[way]
        return remote(part, part, up_send.at[0], up_recv.at[way, hop + step - 1, piece], device)

    def up_sends(way, hop, piece):
        if hop < EXPAND_LATE:
            steps = (1,)
        elif (hop - EXPAND_LATE) % 2 == 0:
            steps = (2, 1)
        else:
            steps = ()
        for step in steps:
            if hop + step < HALF or (hop + step == HALF and piece == way):
                yield up_copy(way, hop, owner_at(way, hop), piece, step)

    def up_forward(way, hop):
        for piece in (way, 1 - way):
            for copy in up_sends(way, hop, piece):
                copy.start()

    def upsib_copy(way, hop, which):
        shard = expands.at[owner_at(way, hop, which), up_part(way, hop)]
        return remote(shard, shard, upsib_send.at[0], upsib_recv.at[0], sibling)

    def up_arrived(hop, turn):
        for way in (0, 1):
            piece = way if turn == 0 else 1 - way
            if hop < HALF or turn == 0:
                up_copy(way, hop - 1, owner_at(way, hop), piece).wait_recv()
                for copy in up_sends(way, hop, piece):
                    copy.start()

    def up_shared(hop):
        for way in (0, 1):
            upsib_copy(way, hop, core).start()

    def up_hop(hop):
        for turn in (0, 1):
            up_arrived(hop, turn)
        up_shared(hop)

    for turn in (0, 1):
        for way in (0, 1):
            piece = way if turn == 0 else 1 - way
            ring_copy(way, 0, piece, shrink_hbm.at[pl.ds(2 * piece, 2)]).start()

    def base_block(pair):
        both = jnp.dot(act[...], kv[:, pl.ds(pl.multiple_of(pair * 2 * FEAT, 2 * FEAT), 2 * FEAT)], preferred_element_type=F32)
        part_out[2 * pair] = both[:, :FEAT].astype(BF16)
        part_out[2 * pair + 1] = both[:, FEAT:].astype(BF16)

    def base_blocks(place):
        if place == 0:
            loads[0].wait()
            loads[1].wait()
        half = PEERS // 4
        lax.fori_loop(place * half, place * half + half, lambda pair, carry: (base_block(pair), carry)[1], 0)

    def base_copy(index):
        offset = OFFSETS[index]
        other_x, other_y = peer(offset)
        return remote(
            part_out.at[other_x * YS + other_y], part_in.at[index], base_send.at[0], base_recv.at[index // 5], peer_id(offset)
        )

    def own_base():
        base[...] = jnp.dot(
            act[...], kv[:, pl.ds(pl.multiple_of(tensor * FEAT, FEAT), FEAT)], preferred_element_type=F32
        )

    def adapters():
        for copy in loads[2:]:
            copy.wait()
        slot_row = slots[...]
        named = jnp.zeros((1, REQ), jnp.int32)
        for slot in range(SLOTS):
            named = jnp.where(slot_row == slot, owners[slot] * HELD + locals_[slot], named)
        adapter[...] = jnp.broadcast_to(named, adapter.shape)
        act_t[...] = act[...].T
        picked[...] = jnp.zeros_like(picked)

    def hot_slots(place):
        slot_column = jnp.broadcast_to(slots[...], (FEAT, REQ)).T
        lane_slot = lax.broadcasted_iota(jnp.int32, (REQ, FEAT), 1) // RANK
        for pair in range(4 * place, 4 * place + 4):
            hot[:, pair * FEAT : (pair + 1) * FEAT] = jnp.where(slot_column == lane_slot + 2 * pair, 1.0, 0.0).astype(BF16)

    def first_work(place):
        if place < 2:
            base_blocks(place)
        elif place == 2:
            for index in range(len(OFFSETS)):
                base_copy(index).start()
            own_base()
        else:
            adapters()
            sib_copy(0, 0, core).start()

    def shrink_with(owner, first=0, count=HELD):
        weights = shrinks[owner, pl.ds(first, count)].reshape(count * RANK, WIDTH)
        block = jnp.dot(weights, act_t[...], preferred_element_type=F32)
        total = picked[...]
        for local in range(count):
            hit = adapter[0:1, :] == owner * HELD + first + local
            total = jnp.where(hit, block[local * RANK : (local + 1) * RANK], total)
        picked[...] = total

    def add_base(index):
        if index % 5 == 0:
            in_bytes(part_in.at[pl.ds(index, 5)], base_recv.at[index // 5]).wait_recv()
        base[...] += part_in[index].astype(F32)

    def work(place, hop):
        way = place % 2
        if place < 2:
            shrink_with(owner_at(way, hop))
        elif way == 0:
            sib_copy(0, hop, 1 - core).wait_recv()
            shrink_with(owner_at(0, hop, 1 - core))
        else:
            sib_copy(1, hop, 1 - core).wait_recv()
            shrink_with(owner_at(1, hop, 1 - core))

    def own_work(place):
        if place == 0:
            shrink_with(dp)
        elif place == 1:
            sib_copy(0, 0, 1 - core).wait_recv()
            shrink_with(sibling["dp"])

    def early(place, hop):
        pl.when(hop == 1)(functools.partial(first_work, place))
        pl.when(hop == 2)(functools.partial(own_work, place))
        pl.when(hop == 3)(functools.partial(hot_slots, place))
        pl.when(hop > 1)(functools.partial(work, place, hop - 1))

    def late(place, hop):
        work(place, hop - 1)

    def shrink_hop(extra, hop, carry):
        for turn in (0, 1):
            for way in (0, 1):
                piece = way if turn == 0 else 1 - way
                ring_arrived(way, hop, piece)
                if turn == 0:
                    ring_forward(way, hop, piece)
                else:
                    pl.when(hop < HALF - 1)(functools.partial(ring_forward, way, hop, piece))
            extra(2 * turn, hop)
            extra(2 * turn + 1, hop)
        for way in (0, 1):
            sib_copy(way, hop, core).start()
        return carry

    lax.fori_loop(1, 5, functools.partial(shrink_hop, early), 0)
    up_forward(0, 0)
    up_forward(1, 0)
    upsib_copy(0, 0, core).start()
    for hop in range(5, HALF):
        shrink_hop(late, hop, 0)
        up_hop(hop - 4)
        for index in range(5 * (hop - 5), 5 * (hop - 4)):
            add_base(index)
    for place in range(HELD):
        work(place, HALF - 1)
    for way in (0, 1):
        ring_arrived(way, HALF, way)
        sib_half(way, core).start()
    up_hop(EXPAND_LATE)
    for way in (0, 1):
        shrink_with(owner_at(way, HALF), 2 * way, 2)
    for way in (0, 1):
        sib_half(way, 1 - core).wait_recv()
        shrink_with(owner_at(way, HALF, 1 - core), 2 * way, 2)

    def piece_of(ref, at_x, at_y):
        return ref.at[pl.ds(pl.multiple_of(at_x * 16, 16), 16), pl.ds(pl.multiple_of(at_y * 128, 128), 128)]

    def sum_copy(index):
        other_x, other_y = peer(OFFSETS[index])
        return remote(
            piece_of(picked, other_x, other_y), sum_in.at[index], sum_send.at[0], sum_recv.at[0], peer_id(OFFSETS[index])
        )

    def all_copy(index):
        return remote(
            piece_of(shrunk_t, x, y), piece_of(shrunk_t, x, y), all_send.at[0], all_recv.at[0],
            peer_id(OFFSETS[index]),
        )

    for index in range(len(OFFSETS)):
        sum_copy(index).start()
    up_arrived(6, 0)
    total = piece_of(picked, x, y)[...]
    in_bytes(sum_in, sum_recv.at[0]).wait_recv()
    for index in range(len(OFFSETS)):
        total += sum_in[index]
    piece_of(shrunk_t, x, y)[...] = total.astype(BF16)
    for index in range(len(OFFSETS)):
        all_copy(index).start()
    up_arrived(6, 1)
    up_shared(6)
    up_hop(5)
    up_hop(7)
    up_hop(HALF)
    in_bytes(all_pieces, all_recv.at[0]).wait_recv()
    twice = jnp.concatenate([shrunk_t[...], shrunk_t[...]], axis=0).T
    for pair in range(SLOTS // 2):
        hot[:, pair * FEAT : (pair + 1) * FEAT] *= twice
    in_bytes(expands.at[pl.ds(0, PLANES)], upsib_recv.at[0]).wait_recv()
    for slot in range(SLOTS):
        rows[slot * RANK : (slot + 1) * RANK, :] = expands[owners[slot], locals_[slot]]
    out[...] = (base[...] + jnp.dot(hot[...], rows[...], preferred_element_type=F32)).astype(BF16)

    chunks = 2 * ((HALF - 1) * HELD + 2)
    in_bytes(shrinks.at[pl.ds(0, chunks // HELD)], ring_send.at[0]).wait_send()
    in_bytes(shrinks.at[pl.ds(0, PLANES)], sib_send.at[0]).wait_send()
    in_bytes(expands.at[pl.ds(0, PLANES - 1)], up_send.at[0]).wait_send()
    in_bytes(expands.at[pl.ds(0, PLANES)], upsib_send.at[0]).wait_send()
    in_bytes(part_in, base_send.at[0]).wait_send()
    in_bytes(sum_in, sum_send.at[0]).wait_send()
    in_bytes(all_pieces, all_send.at[0]).wait_send()


def shards(activations, kv_weight, pool_shrink, pool_expand, request_slot, slot_owner, slot_local):
    peers = len(OFFSETS)
    dma = pltpu.SemaphoreType.DMA
    hbm = pl.BlockSpec(memory_space=pltpu.HBM)
    vmem = pl.BlockSpec(memory_space=pltpu.VMEM)
    return pl.pallas_call(
        kernel,
        out_shape=jax.ShapeDtypeStruct((REQ, FEAT), BF16),
        in_specs=[hbm] * 7,
        out_specs=vmem,
        scratch_shapes=[
            pltpu.SMEM((SLOTS,), jnp.int32),
            pltpu.SMEM((SLOTS,), jnp.int32),
            pltpu.VMEM((1, REQ), jnp.int32),
            pltpu.VMEM((REQ, WIDTH), BF16),
            pltpu.VMEM((WIDTH, REQ), BF16),
            pltpu.VMEM((WIDTH, PEERS * FEAT), BF16),
            pltpu.VMEM((OWNERS, HELD, RANK, WIDTH), BF16),
            pltpu.VMEM((OWNERS, HELD, RANK, FEAT), BF16),
            pltpu.VMEM((PEERS, REQ, FEAT), BF16),
            pltpu.VMEM((peers, REQ, FEAT), BF16),
            pltpu.VMEM((REQ, FEAT), F32),
            pltpu.VMEM((8, REQ), jnp.int32),
            pltpu.VMEM((RANK, REQ), F32),
            pltpu.VMEM((peers, 16, 128), F32),
            pltpu.VMEM((RANK, REQ), BF16),
            pltpu.VMEM((REQ, SLOTS * RANK), BF16),
            pltpu.VMEM((SLOTS * RANK, FEAT), BF16),
            dma((7,)),
            dma((1,)),
            dma((2, HALF, 2)),
            dma((1,)),
            dma((2, HALF + 1)),
            dma((1,)),
            dma((2, HALF, 2)),
            dma((1,)),
            dma((1,)),
            dma((1,)),
            dma((3,)),
            dma((1,)),
            dma((1,)),
            dma((1,)),
            dma((1,)),
        ],
        compiler_params=pltpu.CompilerParams(
            collective_id=0, has_side_effects=True, vmem_limit_bytes=60 * 2**20
        ),
    )(
        slot_owner.reshape(-1), slot_local.reshape(-1), request_slot.reshape(1, -1),
        activations, kv_weight, pool_shrink, pool_expand,
    )


def solution(mesh):
    in_specs = (
        P("dp", "tensor"),
        P("tensor", None),
        P("dp", None, "tensor"),
        P("dp", None, "tensor"),
        P("dp"),
        P("dp", None),
        P("dp", None),
    )
    out_specs = P("dp", "tensor")
    return jax.shard_map(shards, mesh=mesh, in_specs=in_specs, out_specs=out_specs, check_vma=False)
```
